32 devices in a mesh: client: 4 (over x, core), tp: 8 (over z, y).
Axes of the slice: x: 2, y: 2, z: 4, core: 2. Of those that a mesh axis runs over, the one named last changes fastest.
Arguments:
- inputs: bfloat16 [4, 128, 2048], P('client'), may hold values from -6 to 6
- targets: bfloat16 [4, 128, 2048], P('client'), may hold values from -6 to 6
- norm_gain: float32 [2048], replicated, may hold values from 0.1 to 1.9
- gate_weight: bfloat16 [2048, 4096], P(None, 'tp'), may hold values from -0.125 to 0.125
- up_weight: bfloat16 [2048, 4096], P(None, 'tp'), may hold values from -0.125 to 0.125
- down_weight: bfloat16 [4096, 2048], P('tp'), may hold values from -0.09375 to 0.09375
- overflow: int32 [4, 3, 8], P('client', None, 'tp'), may hold values 0 or 1
Outputs:
- gate_update: float32 [2048, 4096], P('client', 'tp')
- up_update: float32 [2048, 4096], P('client', 'tp')
- down_update: float32 [4096, 2048], P('tp', 'client')
- gain_update: float32 [2048], P('client')
The draws below stay inside these ranges and needn't reach their ends.
All inputs are finite; a program needn't handle non-finite values. No bound on the sum of `overflow` on one device may be relied on, other than what follows from the above.
Results may differ from the reference program's by a relative error of at most 0.014.
Values may be sent and summed in bfloat16 or wider, within the bound.
A program may use at most 128 MiB of HBM per device.

```python
import math
import jax
import jax.numpy as jnp
from jax import lax

D = 2048
FF = 4096
TOK_DEV = 128
STEPS = 3
CLIENTS = 4
N_TP = 8


def set_ends(drawn, own_key, low, high):
    shape = drawn.shape
    place = [jax.random.randint(jax.random.fold_in(own_key, axis), (), 0, shape[axis]) for axis in range(len(shape))]
    drawn = drawn.at[tuple(place)].set(low)
    longest = shape.index(max(shape))
    place[longest] = (place[longest] + 1) % shape[longest]
    return drawn.at[tuple(place)].set(high)


def level_of(own_key, dims, shards, low, largest):
    loudness, own = 1.0, jax.random.fold_in(own_key, 6)
    for dim, blocks in shards:
        draws = jnp.exp(jax.random.uniform(jax.random.fold_in(own, dim), (blocks,), jnp.float32, low / len(shards), largest / len(shards)))
        loudness = loudness * jnp.repeat(draws, dims[dim] // blocks).reshape([-1 if axis == dim else 1 for axis in range(len(dims))])
    return loudness


def normal_values(own_key, extent, scale, reach, split=(), dtype=jnp.bfloat16):
    result = jax.random.normal(own_key, extent, jnp.float32) * scale
    if len(split) > 0:
        result = level_of(own_key, extent, split, -0.22, 0.18) * result
    return jnp.clip(result, min=-reach, max=reach).astype(dtype)


def setup_inputs(seed: int = 0) -> dict:
    arg_keys = jax.random.split(jax.random.key(seed), 8)
    return {
        "inputs": normal_values(arg_keys[0], (CLIENTS, TOK_DEV, D), 1.0, 6.0, ((0, 4),)),
        "targets": normal_values(arg_keys[1], (CLIENTS, TOK_DEV, D), 1.0, 6.0, ((0, 4),)),
        "norm_gain": jnp.clip(1.0 + 0.18 * jax.random.normal(arg_keys[2], (D,), jnp.float32), 0.1, 1.9),
        "gate_weight": normal_values(arg_keys[3], (D, FF), D ** -0.5, 0.125, ((1, 8),)),
        "up_weight": normal_values(arg_keys[4], (D, FF), D ** -0.5, 0.125, ((1, 8),)),
        "down_weight": normal_values(arg_keys[5], (FF, D), FF ** -0.5, 0.09375, ((0, 8),)),
        "overflow": set_ends((jax.random.randint(arg_keys[6], (CLIENTS, STEPS, N_TP), 0, 64) < 1).astype(jnp.int32), jax.random.fold_in(arg_keys[6], 1), 0, 1),
    }


def client_round(features, target_rows, flag_rows, norm_gain, gate_weight, up_weight, down_weight):
    limit = 0.5 * math.sqrt(3.0 * D * FF)
    activ = features.astype(jnp.float32)
    scaled = activ * lax.rsqrt(lax.optimization_barrier(jnp.mean(activ * activ, axis=-1, keepdims=True)) + 1e-05)
    gain_master = norm_gain.astype(jnp.float32)
    gate_master = gate_weight.astype(jnp.float32)
    up_master = up_weight.astype(jnp.float32)
    down_master = down_weight.astype(jnp.float32)
    gate_total = jnp.zeros_like(gate_master)
    up_total = jnp.zeros_like(up_master)
    down_total = jnp.zeros_like(down_master)
    gain_total = jnp.zeros_like(gain_master)
    for local_step in range(STEPS):
        normed = (scaled * gain_master).astype(jnp.bfloat16)
        gate_copy = gate_master.astype(jnp.bfloat16)
        up_copy = up_master.astype(jnp.bfloat16)
        down_copy = down_master.astype(jnp.bfloat16)
        gate_act = jnp.dot(normed, gate_copy, preferred_element_type=jnp.float32)
        up_act = jnp.dot(normed, up_copy, preferred_element_type=jnp.float32)
        sig_gate = jax.nn.sigmoid(gate_act)
        silu_gate = gate_act * sig_gate
        hidden = (silu_gate * up_act).astype(jnp.bfloat16)
        outputs = activ + jnp.dot(hidden, down_copy, preferred_element_type=jnp.float32)
        grad_out = (outputs - target_rows.astype(jnp.float32)).astype(jnp.bfloat16)
        grad_down = jnp.dot(hidden.T, grad_out, preferred_element_type=jnp.float32)
        grad_hidden = jnp.dot(grad_out, down_copy.T, preferred_element_type=jnp.float32)
        grad_gate_act = (grad_hidden * up_act * (sig_gate * (1.0 + gate_act * (1.0 - sig_gate)))).astype(jnp.bfloat16)
        grad_up_act = (grad_hidden * silu_gate).astype(jnp.bfloat16)
        grad_gate = jnp.dot(normed.T, grad_gate_act, preferred_element_type=jnp.float32)
        grad_up = jnp.dot(normed.T, grad_up_act, preferred_element_type=jnp.float32)
        grad_normed = jnp.dot(grad_gate_act, gate_copy.T, preferred_element_type=jnp.float32)
        grad_normed = grad_normed + jnp.dot(grad_up_act, up_copy.T, preferred_element_type=jnp.float32)
        grad_gain = lax.optimization_barrier(jnp.sum(grad_normed * scaled, axis=0))
        squares = jnp.sum(grad_gate * grad_gate) + jnp.sum(grad_up * grad_up) + jnp.sum(grad_down * grad_down)
        squares = squares + jnp.sum(grad_gain * grad_gain)
        grad_norm = jnp.sqrt(squares + 1e-06)
        flagged = jnp.sum(flag_rows[local_step])
        factor = jnp.where(flagged == 0, limit / jnp.maximum(grad_norm, limit), 0.0)
        gate_master = gate_master - 0.005 * factor * grad_gate
        up_master = up_master - 0.005 * factor * grad_up
        down_master = down_master - 0.005 * factor * grad_down
        gain_master = gain_master - 0.005 * factor * grad_gain
        gate_total = gate_total + factor * grad_gate
        up_total = up_total + factor * grad_up
        down_total = down_total + factor * grad_down
        gain_total = gain_total + factor * grad_gain
    return (gate_total, up_total, down_total, gain_total)

def reference(inputs, targets, norm_gain, gate_weight, up_weight, down_weight, overflow):

    def visit(carry, items):
        features, target_rows, flag_rows = items
        totals = client_round(features, target_rows, flag_rows, norm_gain, gate_weight, up_weight, down_weight)
        return (tuple((a + b for a, b in zip(carry, totals))), None)
    start = (jnp.zeros((D, FF), jnp.float32), jnp.zeros((D, FF), jnp.float32), jnp.zeros((FF, D), jnp.float32), jnp.zeros((D,), jnp.float32))
    sums, unused = lax.scan(visit, start, (inputs, targets, overflow))
    return (sums[0] / CLIENTS, sums[1] / CLIENTS, sums[2] / CLIENTS, sums[3] / CLIENTS)
```

```python
import functools
import math

import jax
import jax.numpy as jnp
from jax import lax
from jax.experimental import pallas as pl
from jax.experimental.pallas import tpu as pltpu
from jax.sharding import PartitionSpec as P

LR = 0.005
F32 = jnp.float32
BF16 = jnp.bfloat16
MESH = pl.DeviceIdType.MESH


def mm(left, right):
    return lax.dot_general(left, right, (((1,), (0,)), ((), ())), preferred_element_type=F32)


def mm_nt(left, right):
    return lax.dot_general(left, right, (((1,), (1,)), ((), ())), preferred_element_type=F32)


def mm_tn(left, right):
    return lax.dot_general(left, right, (((0,), (0,)), ((), ())), preferred_element_type=F32)


def sum_all(value):
    return jnp.sum(jnp.sum(value, axis=0, keepdims=True), axis=1, keepdims=True)


def kernel(
    n_tp, n_cl, steps, limit,
    x_ref, t_ref, gain_ref, wg_ref, wu_ref, wd_ref, flag_ref,
    og_ref, ou_ref, od_ref, ogain_ref,
    scaled, gain, n_buf, o_buf, part, rs_buf, sm_buf, n_cli, o_cli, h_cli, g_cli, fin,
    ga, ua, sg, gh, hh, oo, coef,
    rs_s, rs_r, ag_s, ag_r, sm_s, sm_r, cn_s, cn_r, ch_s, ch_r, co_s, co_r, cg_s, cg_r, fi_s, fi_r,
):
    tp = lax.axis_index("tp")
    cl = lax.axis_index("client")
    tok, width = x_ref.shape
    dt = width // n_tp
    ds = width // n_cl
    q = ds // dt

    def tp_peer(k):
        return lax.rem(tp + k, n_tp)

    def cl_peer(k):
        return lax.rem(cl + k, n_cl)

    barrier = pltpu.get_barrier_semaphore()

    @pl.loop(1, n_tp)
    def _(k):
        pl.semaphore_signal(barrier, inc=1, device_id={"tp": tp_peer(k)}, device_id_type=MESH)

    @pl.loop(1, n_cl)
    def _(k):
        pl.semaphore_signal(barrier, inc=1, device_id={"client": cl_peer(k)}, device_id_type=MESH)

    def lanes(p):
        return pl.ds(pl.multiple_of(p * dt, dt), dt)

    def slice_of(c):
        return pl.ds(pl.multiple_of(c * ds, ds), ds)

    def tp_copy(src, dst, send, recv, k):
        return pltpu.make_async_remote_copy(
            src_ref=src, dst_ref=dst, send_sem=send, recv_sem=recv,
            device_id={"tp": tp_peer(k)}, device_id_type=MESH)

    def cl_copy(src, dst, send, recv, k):
        return pltpu.make_async_remote_copy(
            src_ref=src, dst_ref=dst, send_sem=send, recv_sem=recv,
            device_id={"client": cl_peer(k)}, device_id_type=MESH)

    def rs_copy(s, k):
        return tp_copy(part.at[tp_peer(k)], rs_buf.at[s, k - 1], rs_s.at[k - 1], rs_r.at[s, k - 1], k)

    def ag_copy(s, k):
        own = o_buf.at[s, :, lanes(tp)]
        return tp_copy(own, own, ag_s.at[k - 1], ag_r.at[s, k - 1], k)

    def ag_arrival(s, k):
        theirs = o_buf.at[s, :, lanes(tp_peer(n_tp - k))]
        return tp_copy(theirs, theirs, ag_s.at[k - 1], ag_r.at[s, k - 1], k)

    def sm_copy(s, k):
        own = sm_buf.at[s, tp]
        return tp_copy(own, own, sm_s.at[k - 1], sm_r.at[s, k - 1], k)

    def sm_arrival(s, k):
        theirs = sm_buf.at[s, tp_peer(n_tp - k)]
        return tp_copy(theirs, theirs, sm_s.at[k - 1], sm_r.at[s, k - 1], k)

    def from_cl(k):
        return cl_peer(n_cl - k)

    def cn_copy(s, k, c):
        return cl_copy(n_buf.at[s, :, slice_of(cl_peer(k))], n_cli.at[s, c], cn_s.at[s, k - 1], cn_r.at[s, k - 1], k)

    def co_copy(s, k, c):
        return cl_copy(o_buf.at[s, :, slice_of(cl_peer(k))], o_cli.at[s, c], co_s.at[s, k - 1], co_r.at[s, k - 1], k)

    def ch_copy(s, k, c):
        return cl_copy(h_cli.at[s, c], h_cli.at[s, c], ch_s.at[s, k - 1], ch_r.at[s, k - 1], k)

    def cg_copy(s, k, c):
        return cl_copy(g_cli.at[:, s, c], g_cli.at[:, s, c], cg_s.at[s, k - 1], cg_r.at[s, k - 1], k)

    def fi_copy(k, c):
        return cl_copy(fin.at[c], fin.at[c], fi_s.at[k - 1], fi_r.at[k - 1], k)

    x = x_ref[...].astype(F32)
    scaled[...] = x * lax.rsqrt(jnp.mean(x * x, axis=-1, keepdims=True) + 1e-05)
    gain[...] = gain_ref[...]
    for p in range(n_tp):
        fin[cl, steps + p] = jnp.zeros((1, dt), F32)

    def step(s, carry):
        for p in range(n_tp):
            at = slice(p * dt, (p + 1) * dt)
            n_buf[s, :, at] = (scaled[:, at] * gain[p]).astype(BF16)

        @pl.when(s == 0)
        def _():
            pl.semaphore_wait(barrier, n_tp - 1 + n_cl - 1)

        @pl.loop(1, n_cl)
        def _(k):
            cn_copy(s, k, cl).start()

        normed = n_buf[s]
        ga[...] = mm(normed, wg_ref[...])
        ua[...] = mm(normed, wu_ref[...])

        @pl.loop(0, s)
        def _(j):
            p = (mm_nt(n_buf[s], n_buf[j]) * coef[j]).astype(BF16)
            ga[...] += mm(p, g_cli[0, j, cl])
            ua[...] += mm(p, g_cli[1, j, cl])

        gate = ga[...]
        sig = jax.nn.sigmoid(gate)
        silu = gate * sig
        sg[...] = sig
        h_cli[s, cl] = (silu * ua[...]).astype(BF16)

        @pl.loop(0, s + 1)
        def _(j):
            hh[j] = mm_nt(h_cli[s, cl], h_cli[j, cl])

        def out_chunk(p):
            first = mm(h_cli[s, cl], wd_ref[:, lanes(p)])

            def more(j, acc):
                return acc + mm((hh[j] * coef[j]).astype(BF16), o_buf[j, :, lanes(p)])

            return lax.fori_loop(0, s, more, first)

        @pl.loop(1, n_tp)
        def _(k):
            part[tp_peer(k)] = out_chunk(tp_peer(k)).astype(BF16)
            rs_copy(s, k).start()

        summed = out_chunk(tp)

        @pl.loop(1, n_cl)
        def _(k):
            ch_copy(s, k, cl).start()

        summed = summed + (x_ref[:, lanes(tp)].astype(F32) - t_ref[:, lanes(tp)].astype(F32))
        for k in range(1, n_tp):
            rs_copy(s, k).wait_recv()
            summed = summed + rs_buf[s, k - 1].astype(F32)
        o_buf[s, :, lanes(tp)] = summed.astype(BF16)

        @pl.loop(1, n_tp)
        def _(k):
            ag_copy(s, k).start()

        gh[...] = mm_nt(o_buf[s, :, lanes(tp)], wd_ref[:, lanes(tp)])
        for k in range(1, n_tp):
            ag_arrival(s, k).wait_recv()
            at = lanes(tp_peer(n_tp - k))
            gh[...] += mm_nt(o_buf[s, :, at], wd_ref[:, at])

        @pl.loop(1, n_cl)
        def _(k):
            co_copy(s, k, cl).start()

        @pl.loop(0, s)
        def _(j):
            p = (mm_nt(o_buf[s], o_buf[j]) * coef[j]).astype(BF16)
            gh[...] += mm(p, h_cli[j, cl])

        oo[...] = mm_nt(o_buf[s], o_buf[s])
        sig = sg[...]
        gate = ga[...]
        grad_hidden = gh[...]
        gg = (grad_hidden * ua[...] * (sig * (1.0 + gate * (1.0 - sig)))).astype(BF16)
        gu = (grad_hidden * (gate * sig)).astype(BF16)
        g_cli[0, s, cl] = gg
        g_cli[1, s, cl] = gu

        @pl.loop(1, n_cl)
        def _(k):
            cg_copy(s, k, cl).start()

        squares = sum_all(mm_nt(n_buf[s], n_buf[s]) * (mm_nt(gg, gg) + mm_nt(gu, gu)) + hh[s] * oo[...])
        sm_buf[s, tp, n_tp] = jnp.broadcast_to(squares, (1, dt))
        sm_buf[s, tp, n_tp + 1] = flag_ref[s]

        @pl.loop(0, s)
        def _(j):
            oo_j = mm_nt(g_cli[0, s, cl], g_cli[0, j, cl]) + mm_nt(g_cli[1, s, cl], g_cli[1, j, cl])
            hh[j] = oo_j * coef[j]

        @pl.loop(0, n_tp)
        def _(p):
            rows = pl.ds(pl.multiple_of(p * dt, dt), dt)
            first = mm_nt(g_cli[0, s, cl], wg_ref[rows, :]) + mm_nt(g_cli[1, s, cl], wu_ref[rows, :])

            def more(j, acc):
                return acc + mm(hh[j].astype(BF16), n_buf[j, :, lanes(p)])

            grad_normed = lax.fori_loop(0, s, more, first)
            sm_buf[s, tp, p] = jnp.sum(grad_normed * scaled[:, lanes(p)], axis=0, keepdims=True)

        @pl.loop(1, n_tp)
        def _(k):
            sm_copy(s, k).start()

        @pl.loop(1, n_tp)
        def _(k):
            rs_copy(s, k).wait_send()
            ag_copy(s, k).wait_send()

        @pl.loop(1, n_tp)
        def _(k):
            sm_arrival(s, k).wait_recv()

        total = sm_buf[s, 0]
        for t in range(1, n_tp):
            total = total + sm_buf[s, t]
        gain_grad = total[:n_tp]
        gain_square = jnp.sum(jnp.sum(gain_grad * gain_grad, axis=0), axis=1, keepdims=True)
        norm = jnp.sqrt(jnp.maximum(total[n_tp], 0.0) + gain_square + 1e-06)
        factor = jnp.where(total[n_tp + 1] < 0.5, limit / jnp.maximum(norm, limit), 0.0)
        fin[cl, s] = factor
        coef[s] = jnp.broadcast_to(factor[:, :tok] * (-LR), (1, tok))
        for p in range(n_tp):
            change = factor * gain_grad[p]
            gain[p] = gain[p] - LR * change
            fin[cl, steps + p] = fin[cl, steps + p] + change

        @pl.loop(1, n_tp)
        def _(k):
            sm_copy(s, k).wait_send()

        n_cli[s, cl] = n_buf[s, :, slice_of(cl)]
        o_cli[s, cl] = o_buf[s, :, slice_of(cl)]
        return carry

    lax.fori_loop(0, steps, step, 0)

    @pl.loop(1, n_cl)
    def _(k):
        fi_copy(k, cl).start()

    @pl.loop(0, steps)
    def _(s):
        @pl.loop(1, n_cl)
        def _(k):
            c = from_cl(k)
            cn_copy(s, k, c).wait_recv()
            ch_copy(s, k, c).wait_recv()
            co_copy(s, k, c).wait_recv()
            cg_copy(s, k, c).wait_recv()
            cn_copy(s, k, cl).wait_send()
            ch_copy(s, k, cl).wait_send()
            co_copy(s, k, cl).wait_send()
            cg_copy(s, k, cl).wait_send()

    @pl.loop(1, n_cl)
    def _(k):
        fi_copy(k, from_cl(k)).wait_recv()
        fi_copy(k, cl).wait_send()

    for i in range(q):
        acc = fin[0, steps + cl * q + i]
        for c in range(1, n_cl):
            acc = acc + fin[c, steps + cl * q + i]
        ogain_ref[i] = acc * (1.0 / n_cl)

    @pl.loop(0, n_cl)
    def _(c):
        @pl.loop(0, steps)
        def _(s):
            f = fin[c, s][:, :1] * (1.0 / n_cl)
            n_cli[s, c] = (n_cli[s, c].astype(F32) * f).astype(BF16)
            o_cli[s, c] = (o_cli[s, c].astype(F32) * f).astype(BF16)

    rows = steps * n_cl * tok
    ff = wg_ref.shape[1]
    n_all = n_cli[...].reshape(rows, ds)
    og_ref[...] = mm_tn(n_all, g_cli[0].reshape(rows, ff))
    ou_ref[...] = mm_tn(n_all, g_cli[1].reshape(rows, ff))
    od_ref[...] = mm_tn(h_cli[...].reshape(rows, ff), o_cli[...].reshape(rows, ds))


def on_device(n_tp, n_cl, inputs, targets, norm_gain, gate_weight, up_weight, down_weight, overflow):
    tok, width = inputs.shape[1:]
    ff = gate_weight.shape[1]
    steps = overflow.shape[1]
    dt = width // n_tp
    ds = width // n_cl
    limit = 0.5 * math.sqrt(3.0 * width * ff * n_tp)
    flags = jnp.broadcast_to(overflow.astype(F32).reshape(steps, 1, 1), (steps, 1, dt))
    gain = norm_gain.reshape(n_tp, 1, dt)
    dma = pltpu.SemaphoreType.DMA
    vmem = pl.BlockSpec(memory_space=pltpu.VMEM)
    gate, up, down, gain_out = pl.pallas_call(
        functools.partial(kernel, n_tp, n_cl, steps, limit),
        out_shape=(
            jax.ShapeDtypeStruct((ds, ff), F32),
            jax.ShapeDtypeStruct((ds, ff), F32),
            jax.ShapeDtypeStruct((ff, ds), F32),
            jax.ShapeDtypeStruct((ds // dt, 1, dt), F32),
        ),
        in_specs=[vmem] * 7,
        out_specs=(vmem,) * 4,
        scratch_shapes=[
            pltpu.VMEM((tok, width), F32),
            pltpu.VMEM((n_tp, 1, dt), F32),
            pltpu.VMEM((steps, tok, width), BF16),
            pltpu.VMEM((steps, tok, width), BF16),
            pltpu.VMEM((n_tp, tok, dt), BF16),
            pltpu.VMEM((steps, n_tp - 1, tok, dt), BF16),
            pltpu.VMEM((steps, n_tp, n_tp + 2, 1, dt), F32),
            pltpu.VMEM((steps, n_cl, tok, ds), BF16),
            pltpu.VMEM((steps, n_cl, tok, ds), BF16),
            pltpu.VMEM((steps, n_cl, tok, ff), BF16),
            pltpu.VMEM((2, steps, n_cl, tok, ff), BF16),
            pltpu.VMEM((n_cl, steps + n_tp, 1, dt), F32),
            pltpu.VMEM((tok, ff), F32),
            pltpu.VMEM((tok, ff), F32),
            pltpu.VMEM((tok, ff), F32),
            pltpu.VMEM((tok, ff), F32),
            pltpu.VMEM((steps, tok, tok), F32),
            pltpu.VMEM((tok, tok), F32),
            pltpu.VMEM((steps, 1, tok), F32),
            dma((n_tp - 1,)), dma((steps, n_tp - 1)),
            dma((n_tp - 1,)), dma((steps, n_tp - 1)),
            dma((n_tp - 1,)), dma((steps, n_tp - 1)),
            dma((steps, n_cl - 1)), dma((steps, n_cl - 1)),
            dma((steps, n_cl - 1)), dma((steps, n_cl - 1)),
            dma((steps, n_cl - 1)), dma((steps, n_cl - 1)),
            dma((steps, n_cl - 1)), dma((steps, n_cl - 1)),
            dma((n_cl - 1,)), dma((n_cl - 1,)),
        ],
        compiler_params=pltpu.CompilerParams(
            collective_id=0, has_side_effects=True, vmem_limit_bytes=48 * 1024 * 1024
        ),
        name="fedavg_round",
    )(inputs[0], targets[0], gain, gate_weight, up_weight, down_weight, flags)
    return gate, up, down, gain_out.reshape(ds)


def solution(mesh):
    placed = (
        P("client", None, None),
        P("client", None, None),
        P(),
        P(None, "tp"),
        P(None, "tp"),
        P("tp", None),
        P("client", None, "tp"),
    )
    return jax.shard_map(
        functools.partial(on_device, mesh.shape["tp"], mesh.shape["client"]),
        mesh=mesh,
        in_specs=placed,
        out_specs=(P("client", "tp"), P("client", "tp"), P("tp", "client"), P("client")),
        check_vma=False,
    )
```

```python
import functools
import math

import jax
import jax.numpy as jnp
from jax import lax
from jax.experimental import pallas as pl
from jax.experimental.pallas import tpu as pltpu
from jax.sharding import PartitionSpec as P

LR = 0.005
F32 = jnp.float32
BF16 = jnp.bfloat16
MESH = pl.DeviceIdType.MESH


def mm(left, right):
    return lax.dot_general(left, right, (((1,), (0,)), ((), ())), preferred_element_type=F32)


def mm_nt(left, right):
    return lax.dot_general(left, right, (((1,), (1,)), ((), ())), preferred_element_type=F32)


def mm_tn(left, right):
    return lax.dot_general(left, right, (((0,), (0,)), ((), ())), preferred_element_type=F32)


def sum_all(value):
    return jnp.sum(jnp.sum(value, axis=0, keepdims=True), axis=1, keepdims=True)


def kernel(
    n_tp, n_cl, steps, limit,
    x_ref, t_ref, gain_ref, wg_ref, wu_ref, wd_ref, flag_ref,
    og_ref, ou_ref, od_ref, ogain_ref,
    scaled, gain, n_buf, o_buf, part, pair_buf, line_buf, sm_buf, n_cli, o_cli, h_cli, g_cli, fin,
    ga, ua, sg, gh, hh, oo, coef,
    rp_s, rp_r, rl_s, rl_r, ap_s, ap_r, al_s, al_r, sm_s, sm_r,
    cn_s, cn_r, ch_s, ch_r, co_s, co_r, cg_s, cg_r, fi_s, fi_r,
):
    tp = lax.axis_index("tp")
    cl = lax.axis_index("client")
    tok, width = x_ref.shape
    dt = width // n_tp
    ds = width // n_cl
    q = ds // dt

    def tp_peer(k):
        return lax.rem(tp + k, n_tp)

    def cl_peer(k):
        return lax.rem(cl + k, n_cl)

    barrier = pltpu.get_barrier_semaphore()

    @pl.loop(1, n_tp)
    def _(k):
        pl.semaphore_signal(barrier, inc=1, device_id={"tp": tp_peer(k)}, device_id_type=MESH)

    @pl.loop(1, n_cl)
    def _(k):
        pl.semaphore_signal(barrier, inc=1, device_id={"client": cl_peer(k)}, device_id_type=MESH)

    def lanes(p):
        return pl.ds(pl.multiple_of(p * dt, dt), dt)

    def slice_of(c):
        return pl.ds(pl.multiple_of(c * ds, ds), ds)

    def tp_copy(src, dst, send, recv, k):
        return pltpu.make_async_remote_copy(
            src_ref=src, dst_ref=dst, send_sem=send, recv_sem=recv,
            device_id={"tp": tp_peer(k)}, device_id_type=MESH)

    def cl_copy(src, dst, send, recv, k):
        return pltpu.make_async_remote_copy(
            src_ref=src, dst_ref=dst, send_sem=send, recv_sem=recv,
            device_id={"client": cl_peer(k)}, device_id_type=MESH)

    line = n_tp // 2
    side = lax.rem(tp, 2)
    spot = lax.div(tp, 2)
    pair = tp + 1 - 2 * side
    sibling = cl + 1 - 2 * lax.rem(cl, 2)
    pairs = n_cl // 2

    def on_line(k):
        return lax.rem(spot + k, line) * 2

    def to_tp(src, dst, send, recv, peer):
        return pltpu.make_async_remote_copy(
            src_ref=src, dst_ref=dst, send_sem=send, recv_sem=recv,
            device_id={"tp": peer}, device_id_type=MESH)

    def to_cl(src, dst, send, recv, peer):
        return pltpu.make_async_remote_copy(
            src_ref=src, dst_ref=dst, send_sem=send, recv_sem=recv,
            device_id={"client": peer}, device_id_type=MESH)

    def rp_copy(s, k):
        return to_tp(part.at[0, k], pair_buf.at[s, k], rp_s.at[k], rp_r.at[s, k], pair)

    def rl_copy(s, k):
        return to_tp(part.at[1, k], line_buf.at[s, k - 1], rl_s.at[k - 1], rl_r.at[s, k - 1], on_line(k) + side)

    def al_copy(s, k, p):
        block = o_buf.at[s, :, lanes(p)]
        return to_tp(block, block, al_s.at[k - 1], al_r.at[s, k - 1], on_line(k) + side)

    def ap_copy(s, k, p):
        block = o_buf.at[s, :, lanes(p)]
        return to_tp(block, block, ap_s.at[k], ap_r.at[s, k], pair)

    def sm_copy(s, k):
        own = sm_buf.at[s, tp]
        return tp_copy(own, own, sm_s.at[k - 1], sm_r.at[s, k - 1], k)

    def sm_arrival(s, k):
        theirs = sm_buf.at[s, tp_peer(n_tp - k)]
        return tp_copy(theirs, theirs, sm_s.at[k - 1], sm_r.at[s, k - 1], k)

    def from_cl(k):
        return cl_peer(n_cl - k)

    def cn_copy(s, k, c):
        return cl_copy(n_buf.at[s, :, slice_of(cl_peer(k))], n_cli.at[s, c], cn_s.at[s, k - 1], cn_r.at[s, k - 1], k)

    def co_copy(s, k, c):
        return cl_copy(o_buf.at[s, :, slice_of(cl_peer(k))], o_cli.at[s, c], co_s.at[s, k - 1], co_r.at[s, k - 1], k)

    def far(m):
        return lax.rem(lax.div(cl, 2) + m, pairs) * 2 + lax.rem(cl, 2)

    def ch_far(s, m, c):
        block = h_cli.at[s, c]
        return to_cl(block, block, ch_s.at[s, m - 1], ch_r.at[s, m - 1], far(m))

    def ch_near(s, m, c):
        block = h_cli.at[s, c]
        return to_cl(block, block, ch_s.at[s, pairs - 1 + m], ch_r.at[s, pairs - 1 + m], sibling)

    def cg_far(s, m, c):
        block = g_cli.at[:, s, c]
        return to_cl(block, block, cg_s.at[s, m - 1], cg_r.at[s, m - 1], far(m))

    def cg_near(s, m, c):
        block = g_cli.at[:, s, c]
        return to_cl(block, block, cg_s.at[s, pairs - 1 + m], cg_r.at[s, pairs - 1 + m], sibling)

    def fi_copy(s, k, c):
        return cl_copy(fin.at[s, c], fin.at[s, c], fi_s.at[s, k - 1], fi_r.at[s, k - 1], k)

    def forward(s):
        for m in range(1, pairs):
            source = far(pairs - m)
            ch_far(s, m, source).wait_recv()
            ch_near(s, m, source).start()
            cg_far(s, m, source).wait_recv()
            cg_near(s, m, source).start()

    def add_out(s):
        for k in range(1, n_cl):
            c = from_cl(k)
            fi_copy(s, k, c).wait_recv()
            cn_copy(s, k, c).wait_recv()
            co_copy(s, k, c).wait_recv()
        for m in range(pairs):
            c = sibling if m == 0 else far(pairs - m) + 1 - 2 * lax.rem(cl, 2)
            ch_near(s, m, c).wait_recv()
            cg_near(s, m, c).wait_recv()
        for c in range(n_cl):
            f = fin[s, c, n_tp][:, :1] * (1.0 / n_cl)
            n_cli[s, c] = (n_cli[s, c].astype(F32) * f).astype(BF16)
            o_cli[s, c] = (o_cli[s, c].astype(F32) * f).astype(BF16)
        rows = n_cl * tok
        ff = wg_ref.shape[1]
        n_all = n_cli[s].reshape(rows, ds)
        og_ref[...] += mm_tn(n_all, g_cli[0, s].reshape(rows, ff))
        ou_ref[...] += mm_tn(n_all, g_cli[1, s].reshape(rows, ff))
        od_ref[...] += mm_tn(h_cli[s].reshape(rows, ff), o_cli[s].reshape(rows, ds))

    x = x_ref[...].astype(F32)
    scaled[...] = x * lax.rsqrt(jnp.mean(x * x, axis=-1, keepdims=True) + 1e-05)
    gain[...] = gain_ref[...]
    og_ref[...] = jnp.zeros_like(og_ref)
    ou_ref[...] = jnp.zeros_like(ou_ref)
    od_ref[...] = jnp.zeros_like(od_ref)

    def step(s, carry):
        for p in range(n_tp):
            at = slice(p * dt, (p + 1) * dt)
            n_buf[s, :, at] = (scaled[:, at] * gain[p]).astype(BF16)

        @pl.when(s == 0)
        def _():
            pl.semaphore_wait(barrier, n_tp - 1 + n_cl - 1)

        @pl.loop(1, n_cl)
        def _(k):
            cn_copy(s, k, cl).start()

        normed = n_buf[s]
        ga[...] = mm(normed, wg_ref[...])
        ua[...] = mm(normed, wu_ref[...])

        @pl.loop(0, s)
        def _(j):
            p = (mm_nt(n_buf[s], n_buf[j]) * coef[j]).astype(BF16)
            ga[...] += mm(p, g_cli[0, j, cl])
            ua[...] += mm(p, g_cli[1, j, cl])

        gate = ga[...]
        sig = jax.nn.sigmoid(gate)
        silu = gate * sig
        sg[...] = sig
        h_cli[s, cl] = (silu * ua[...]).astype(BF16)

        @pl.loop(0, s + 1)
        def _(j):
            hh[j] = mm_nt(h_cli[s, cl], h_cli[j, cl])

        def out_chunk(p):
            first = mm(h_cli[s, cl], wd_ref[:, lanes(p)])

            def more(j, acc):
                return acc + mm((hh[j] * coef[j]).astype(BF16), o_buf[j, :, lanes(p)])

            return lax.fori_loop(0, s, more, first)

        order = list(range(1, line)) + [0]
        for k in order:
            part[0, k] = out_chunk(on_line(k) + 1 - side).astype(BF16)
            rp_copy(s, k).start()
        for k in order:
            summed = out_chunk(on_line(k) + side)
            rp_copy(s, k).wait_recv()
            summed = summed + pair_buf[s, k].astype(F32)
            if k > 0:
                part[1, k] = summed.astype(BF16)
                rl_copy(s, k).start()

        summed = summed + (x_ref[:, lanes(tp)].astype(F32) - t_ref[:, lanes(tp)].astype(F32))
        ch_near(s, 0, cl).start()
        for m in range(1, pairs):
            ch_far(s, m, cl).start()

        @pl.when(s > 0)
        def _():
            forward(s - 1)

        for k in range(1, line):
            rl_copy(s, k).wait_recv()
            summed = summed + line_buf[s, k - 1].astype(F32)
        o_buf[s, :, lanes(tp)] = summed.astype(BF16)

        ap_copy(s, 0, tp).start()
        for k in range(1, line):
            al_copy(s, k, tp).start()

        gh[...] = mm_nt(o_buf[s, :, lanes(tp)], wd_ref[:, lanes(tp)])

        @pl.when(s > 0)
        def _():
            add_out(s - 1)

        for k in range(1, line):
            source = on_line(line - k) + side
            al_copy(s, k, source).wait_recv()
            ap_copy(s, k, source).start()
            at = lanes(source)
            gh[...] += mm_nt(o_buf[s, :, at], wd_ref[:, at])
        for k in range(line):
            source = on_line(line - k) + 1 - side
            ap_copy(s, k, source).wait_recv()
            at = lanes(source)
            gh[...] += mm_nt(o_buf[s, :, at], wd_ref[:, at])

        @pl.loop(1, n_cl)
        def _(k):
            co_copy(s, k, cl).start()

        @pl.loop(0, s)
        def _(j):
            p = (mm_nt(o_buf[s], o_buf[j]) * coef[j]).astype(BF16)
            gh[...] += mm(p, h_cli[j, cl])

        oo[...] = mm_nt(o_buf[s], o_buf[s])
        sig = sg[...]
        gate = ga[...]
        grad_hidden = gh[...]
        gg = (grad_hidden * ua[...] * (sig * (1.0 + gate * (1.0 - sig)))).astype(BF16)
        gu = (grad_hidden * (gate * sig)).astype(BF16)
        g_cli[0, s, cl] = gg
        g_cli[1, s, cl] = gu

        cg_near(s, 0, cl).start()
        for m in range(1, pairs):
            cg_far(s, m, cl).start()

        squares = sum_all(mm_nt(n_buf[s], n_buf[s]) * (mm_nt(gg, gg) + mm_nt(gu, gu)) + hh[s] * oo[...])
        sm_buf[s, tp, n_tp] = jnp.broadcast_to(squares, (1, dt))
        sm_buf[s, tp, n_tp + 1] = flag_ref[s]

        @pl.loop(0, s)
        def _(j):
            oo_j = mm_nt(g_cli[0, s, cl], g_cli[0, j, cl]) + mm_nt(g_cli[1, s, cl], g_cli[1, j, cl])
            hh[j] = oo_j * coef[j]

        @pl.loop(0, n_tp)
        def _(p):
            rows = pl.ds(pl.multiple_of(p * dt, dt), dt)
            first = mm_nt(g_cli[0, s, cl], wg_ref[rows, :]) + mm_nt(g_cli[1, s, cl], wu_ref[rows, :])

            def more(j, acc):
                return acc + mm(hh[j].astype(BF16), n_buf[j, :, lanes(p)])

            grad_normed = lax.fori_loop(0, s, more, first)
            sm_buf[s, tp, p] = jnp.sum(grad_normed * scaled[:, lanes(p)], axis=0, keepdims=True)

        @pl.loop(1, n_tp)
        def _(k):
            sm_copy(s, k).start()

        for k in range(line):
            rp_copy(s, k).wait_send()
            ap_copy(s, k, tp).wait_send()
        for k in range(1, line):
            rl_copy(s, k).wait_send()
            al_copy(s, k, tp).wait_send()

        @pl.loop(1, n_tp)
        def _(k):
            sm_arrival(s, k).wait_recv()

        total = sm_buf[s, 0]
        for t in range(1, n_tp):
            total = total + sm_buf[s, t]
        gain_grad = total[:n_tp]
        gain_square = jnp.sum(jnp.sum(gain_grad * gain_grad, axis=0), axis=1, keepdims=True)
        norm = jnp.sqrt(jnp.maximum(total[n_tp], 0.0) + gain_square + 1e-06)
        factor = jnp.where(total[n_tp + 1] < 0.5, limit / jnp.maximum(norm, limit), 0.0)
        fin[s, cl, n_tp] = factor
        coef[s] = jnp.broadcast_to(factor[:, :tok] * (-LR), (1, tok))
        for p in range(n_tp):
            change = factor * gain_grad[p]
            gain[p] = gain[p] - LR * change
            fin[s, cl, p] = change

        @pl.loop(1, n_cl)
        def _(k):
            fi_copy(s, k, cl).start()

        @pl.loop(1, n_tp)
        def _(k):
            sm_copy(s, k).wait_send()

        n_cli[s, cl] = n_buf[s, :, slice_of(cl)]
        o_cli[s, cl] = o_buf[s, :, slice_of(cl)]
        return carry

    lax.fori_loop(0, steps, step, 0)

    forward(steps - 1)
    add_out(steps - 1)
    for i in range(q):
        acc = jnp.zeros((1, dt), F32)
        for s in range(steps):
            for c in range(n_cl):
                acc = acc + fin[s, c, cl * q + i]
        ogain_ref[i] = acc * (1.0 / n_cl)

    @pl.loop(0, steps)
    def _(s):
        @pl.loop(1, n_cl)
        def _(k):
            cn_copy(s, k, cl).wait_send()
            co_copy(s, k, cl).wait_send()
            fi_copy(s, k, cl).wait_send()

        for m in range(pairs):
            ch_near(s, m, cl).wait_send()
            cg_near(s, m, cl).wait_send()
        for m in range(1, pairs):
            ch_far(s, m, cl).wait_send()
            cg_far(s, m, cl).wait_send()


def on_device(n_tp, n_cl, inputs, targets, norm_gain, gate_weight, up_weight, down_weight, overflow):
    tok, width = inputs.shape[1:]
    ff = gate_weight.shape[1]
    steps = overflow.shape[1]
    dt = width // n_tp
    ds = width // n_cl
    line = n_tp // 2
    limit = 0.5 * math.sqrt(3.0 * width * ff * n_tp)
    flags = jnp.broadcast_to(overflow.astype(F32).reshape(steps, 1, 1), (steps, 1, dt))
    gain = norm_gain.reshape(n_tp, 1, dt)
    dma = pltpu.SemaphoreType.DMA
    vmem = pl.BlockSpec(memory_space=pltpu.VMEM)
    gate, up, down, gain_out = pl.pallas_call(
        functools.partial(kernel, n_tp, n_cl, steps, limit),
        out_shape=(
            jax.ShapeDtypeStruct((ds, ff), F32),
            jax.ShapeDtypeStruct((ds, ff), F32),
            jax.ShapeDtypeStruct((ff, ds), F32),
            jax.ShapeDtypeStruct((ds // dt, 1, dt), F32),
        ),
        in_specs=[vmem] * 7,
        out_specs=(vmem,) * 4,
        scratch_shapes=[
            pltpu.VMEM((tok, width), F32),
            pltpu.VMEM((n_tp, 1, dt), F32),
            pltpu.VMEM((steps, tok, width), BF16),
            pltpu.VMEM((steps, tok, width), BF16),
            pltpu.VMEM((2, line, tok, dt), BF16),
            pltpu.VMEM((steps, line, tok, dt), BF16),
            pltpu.VMEM((steps, line - 1, tok, dt), BF16),
            pltpu.VMEM((steps, n_tp, n_tp + 2, 1, dt), F32),
            pltpu.VMEM((steps, n_cl, tok, ds), BF16),
            pltpu.VMEM((steps, n_cl, tok, ds), BF16),
            pltpu.VMEM((steps, n_cl, tok, ff), BF16),
            pltpu.VMEM((2, steps, n_cl, tok, ff), BF16),
            pltpu.VMEM((steps, n_cl, n_tp + 1, 1, dt), F32),
            pltpu.VMEM((tok, ff), F32),
            pltpu.VMEM((tok, ff), F32),
            pltpu.VMEM((tok, ff), F32),
            pltpu.VMEM((tok, ff), F32),
            pltpu.VMEM((steps, tok, tok), F32),
            pltpu.VMEM((tok, tok), F32),
            pltpu.VMEM((steps, 1, tok), F32),
            dma((line,)), dma((steps, line)),
            dma((line - 1,)), dma((steps, line - 1)),
            dma((line,)), dma((steps, line)),
            dma((line - 1,)), dma((steps, line - 1)),
            dma((n_tp - 1,)), dma((steps, n_tp - 1)),
            dma((steps, n_cl - 1)), dma((steps, n_cl - 1)),
            dma((steps, n_cl - 1)), dma((steps, n_cl - 1)),
            dma((steps, n_cl - 1)), dma((steps, n_cl - 1)),
            dma((steps, n_cl - 1)), dma((steps, n_cl - 1)),
            dma((steps, n_cl - 1)), dma((steps, n_cl - 1)),
        ],
        compiler_params=pltpu.CompilerParams(
            collective_id=0, has_side_effects=True, vmem_limit_bytes=48 * 1024 * 1024
        ),
        name="fedavg_round",
    )(inputs[0], targets[0], gain, gate_weight, up_weight, down_weight, flags)
    return gate, up, down, gain_out.reshape(ds)


def solution(mesh):
    placed = (
        P("client", None, None),
        P("client", None, None),
        P(),
        P(None, "tp"),
        P(None, "tp"),
        P("tp", None),
        P("client", None, "tp"),
    )
    return jax.shard_map(
        functools.partial(on_device, mesh.shape["tp"], mesh.shape["client"]),
        mesh=mesh,
        in_specs=placed,
        out_specs=(P("client", "tp"), P("client", "tp"), P("tp", "client"), P("client")),
        check_vma=False,
    )
```

```python
import functools
import math

import jax
import jax.numpy as jnp
from jax import lax
from jax.experimental import pallas as pl
from jax.experimental.pallas import tpu as pltpu
from jax.sharding import PartitionSpec as P

LR = 0.005
F32 = jnp.float32
BF16 = jnp.bfloat16
MESH = pl.DeviceIdType.MESH


def mm(left, right):
    return lax.dot_general(left, right, (((1,), (0,)), ((), ())), preferred_element_type=F32)


def mm_nt(left, right):
    return lax.dot_general(left, right, (((1,), (1,)), ((), ())), preferred_element_type=F32)


def mm_tn(left, right):
    return lax.dot_general(left, right, (((0,), (0,)), ((), ())), preferred_element_type=F32)


def sum_all(value):
    return jnp.sum(jnp.sum(value, axis=0, keepdims=True), axis=1, keepdims=True)


def kernel(
    n_tp, n_cl, steps, limit,
    x_ref, t_ref, gain_ref, wg_hbm, wu_hbm, wd_hbm, flag_ref,
    og_ref, ou_ref, od_ref, ogain_ref,
    wg_ref, wu_ref, wd_ref, load, o_hist,
    scaled, gain, n_buf, o_buf, part, pair_buf, line_buf, sm_buf, n_cli, o_cli, h_cli, g_cli, fin,
    ga, ua, sg, gh, nn, hh, oo, oh, coef,
    rp_s, rp_r, rl_s, rl_r, ap_s, ap_r, al_s, al_r, sm_s, sm_r,
    cn_s, cn_r, ch_s, ch_r, co_s, co_r, cg_s, cg_r, fi_s, fi_r,
):
    tp = lax.axis_index("tp")
    cl = lax.axis_index("client")
    tok, width = x_ref.shape
    dt = width // n_tp
    ds = width // n_cl
    q = ds // dt

    def tp_peer(k):
        return lax.rem(tp + k, n_tp)

    def cl_peer(k):
        return lax.rem(cl + k, n_cl)

    loads = [
        pltpu.make_async_copy(src, dst, load.at[i])
        for i, (src, dst) in enumerate(((wg_hbm, wg_ref), (wu_hbm, wu_ref), (wd_hbm, wd_ref)))
    ]
    for copy in loads:
        copy.start()
    barrier = pltpu.get_barrier_semaphore()

    @pl.loop(1, n_tp)
    def _(k):
        pl.semaphore_signal(barrier, inc=1, device_id={"tp": tp_peer(k)}, device_id_type=MESH)

    @pl.loop(1, n_cl)
    def _(k):
        pl.semaphore_signal(barrier, inc=1, device_id={"client": cl_peer(k)}, device_id_type=MESH)

    def lanes(p):
        return pl.ds(pl.multiple_of(p * dt, dt), dt)

    def slice_of(c):
        return pl.ds(pl.multiple_of(c * ds, ds), ds)

    def tp_copy(src, dst, send, recv, k):
        return pltpu.make_async_remote_copy(
            src_ref=src, dst_ref=dst, send_sem=send, recv_sem=recv,
            device_id={"tp": tp_peer(k)}, device_id_type=MESH)

    def cl_copy(src, dst, send, recv, k):
        return pltpu.make_async_remote_copy(
            src_ref=src, dst_ref=dst, send_sem=send, recv_sem=recv,
            device_id={"client": cl_peer(k)}, device_id_type=MESH)

    line = n_tp // 2
    side = lax.rem(tp, 2)
    spot = lax.div(tp, 2)
    pair = tp + 1 - 2 * side
    sibling = cl + 1 - 2 * lax.rem(cl, 2)
    pairs = n_cl // 2

    def on_line(k):
        return lax.rem(spot + k, line) * 2

    def to_tp(src, dst, send, recv, peer):
        return pltpu.make_async_remote_copy(
            src_ref=src, dst_ref=dst, send_sem=send, recv_sem=recv,
            device_id={"tp": peer}, device_id_type=MESH)

    def to_cl(src, dst, send, recv, peer):
        return pltpu.make_async_remote_copy(
            src_ref=src, dst_ref=dst, send_sem=send, recv_sem=recv,
            device_id={"client": peer}, device_id_type=MESH)

    def rp_copy(s, k):
        return to_tp(part.at[0, k], pair_buf.at[s, k], rp_s.at[k], rp_r.at[s, k], pair)

    def rl_copy(s, k):
        return to_tp(part.at[1, k], line_buf.at[s, k - 1], rl_s.at[k - 1], rl_r.at[s, k - 1], on_line(k) + side)

    def al_copy(s, k, p):
        block = o_buf.at[s, :, lanes(p)]
        return to_tp(block, block, al_s.at[k - 1], al_r.at[s, k - 1], on_line(k) + side)

    def ap_copy(s, k, p):
        block = o_buf.at[s, :, lanes(p)]
        return to_tp(block, block, ap_s.at[k], ap_r.at[s, k], pair)

    def sm_copy(s, k):
        own = sm_buf.at[s, tp]
        return tp_copy(own, own, sm_s.at[k - 1], sm_r.at[s, k - 1], k)

    def sm_arrival(s, k):
        theirs = sm_buf.at[s, tp_peer(n_tp - k)]
        return tp_copy(theirs, theirs, sm_s.at[k - 1], sm_r.at[s, k - 1], k)

    def from_cl(k):
        return cl_peer(n_cl - k)

    def cn_copy(s, k, c):
        return cl_copy(n_buf.at[s, :, slice_of(cl_peer(k))], n_cli.at[s, c], cn_s.at[s, k - 1], cn_r.at[s, k - 1], k)

    def co_copy(s, k, c):
        return cl_copy(o_buf.at[s, :, slice_of(cl_peer(k))], o_cli.at[s, c], co_s.at[s, k - 1], co_r.at[s, k - 1], k)

    def far(m):
        return lax.rem(lax.div(cl, 2) + m, pairs) * 2 + lax.rem(cl, 2)

    def ch_far(s, m, c):
        block = h_cli.at[s, c]
        return to_cl(block, block, ch_s.at[s, m - 1], ch_r.at[s, m - 1], far(m))

    def ch_near(s, m, c):
        block = h_cli.at[s, c]
        return to_cl(block, block, ch_s.at[s, pairs - 1 + m], ch_r.at[s, pairs - 1 + m], sibling)

    def cg_far(s, m, c):
        block = g_cli.at[:, s, c]
        return to_cl(block, block, cg_s.at[s, m - 1], cg_r.at[s, m - 1], far(m))

    def cg_near(s, m, c):
        block = g_cli.at[:, s, c]
        return to_cl(block, block, cg_s.at[s, pairs - 1 + m], cg_r.at[s, pairs - 1 + m], sibling)

    def fi_copy(s, k, c):
        return cl_copy(fin.at[s, c], fin.at[s, c], fi_s.at[s, k - 1], fi_r.at[s, k - 1], k)

    def forward(s):
        for m in range(1, pairs):
            source = far(pairs - m)
            ch_far(s, m, source).wait_recv()
            ch_near(s, m, source).start()
            cg_far(s, m, source).wait_recv()
            cg_near(s, m, source).start()

    def add_out(s):
        for k in range(1, n_cl):
            c = from_cl(k)
            fi_copy(s, k, c).wait_recv()
            cn_copy(s, k, c).wait_recv()
            co_copy(s, k, c).wait_recv()
        for m in range(pairs):
            c = sibling if m == 0 else far(pairs - m) + 1 - 2 * lax.rem(cl, 2)
            ch_near(s, m, c).wait_recv()
            cg_near(s, m, c).wait_recv()
        for c in range(n_cl):
            f = fin[s, c, n_tp][:, :1] * (1.0 / n_cl)
            n_cli[s, c] = (n_cli[s, c].astype(F32) * f).astype(BF16)
            o_cli[s, c] = (o_cli[s, c].astype(F32) * f).astype(BF16)
        rows = n_cl * tok
        ff = wg_ref.shape[1]
        n_all = n_cli[s].reshape(rows, ds)
        og_ref[...] += mm_tn(n_all, g_cli[0, s].reshape(rows, ff))
        ou_ref[...] += mm_tn(n_all, g_cli[1, s].reshape(rows, ff))
        od_ref[...] += mm_tn(h_cli[s].reshape(rows, ff), o_cli[s].reshape(rows, ds))

    x = x_ref[...].astype(F32)
    scaled[...] = x * lax.rsqrt(jnp.mean(x * x, axis=-1, keepdims=True) + 1e-05)
    gain[...] = gain_ref[...]
    og_ref[...] = jnp.zeros_like(og_ref)
    ou_ref[...] = jnp.zeros_like(ou_ref)
    od_ref[...] = jnp.zeros_like(od_ref)
    past = steps - 1
    rows = past * tok
    ff = wg_ref.shape[1]
    coef[...] = jnp.zeros_like(coef)
    o_hist[...] = jnp.zeros_like(o_hist)
    for j in range(past):
        n_buf[j] = jnp.zeros((tok, width), BF16)
        h_cli[j, cl] = jnp.zeros((tok, ff), BF16)
        g_cli[0, j, cl] = jnp.zeros((tok, ff), BF16)
        g_cli[1, j, cl] = jnp.zeros((tok, ff), BF16)
    for copy in loads:
        copy.wait()

    def h_past():
        return h_cli[:past, cl].reshape(rows, ff)

    def g_past(i):
        return g_cli[i, :past, cl].reshape(rows, ff)

    def step(s, carry):
        for p in range(n_tp):
            at = slice(p * dt, (p + 1) * dt)
            n_buf[s, :, at] = (scaled[:, at] * gain[p]).astype(BF16)

        @pl.when(s == 0)
        def _():
            pl.semaphore_wait(barrier, n_tp - 1 + n_cl - 1)

        @pl.loop(1, n_cl)
        def _(k):
            cn_copy(s, k, cl).start()

        normed = n_buf[s]
        ga[...] = mm(normed, wg_ref[...])
        ua[...] = mm(normed, wu_ref[...])

        @pl.when(s > 0)
        def _():
            p = (mm_nt(n_buf[s], n_buf[:past].reshape(rows, width)) * coef[...]).astype(BF16)
            ga[...] += mm(p, g_past(0))
            ua[...] += mm(p, g_past(1))

        gate = ga[...]
        sig = jax.nn.sigmoid(gate)
        silu = gate * sig
        sg[...] = sig
        hidden = (silu * ua[...]).astype(BF16)
        h_cli[s, cl] = hidden
        p_h = (mm_nt(hidden, h_past()) * coef[...]).astype(BF16)

        def out_chunk(p):
            at = lanes(p)
            return mm(hidden, wd_ref[:, at]) + mm(p_h, o_hist[:, :, at].reshape(rows, dt))

        order = list(range(1, line)) + [0]
        for k in order:
            part[0, k] = out_chunk(on_line(k) + 1 - side).astype(BF16)
            rp_copy(s, k).start()
        for k in order:
            summed = out_chunk(on_line(k) + side)
            rp_copy(s, k).wait_recv()
            summed = summed + pair_buf[s, k].astype(F32)
            if k > 0:
                part[1, k] = summed.astype(BF16)
                rl_copy(s, k).start()

        summed = summed + (x_ref[:, lanes(tp)].astype(F32) - t_ref[:, lanes(tp)].astype(F32))
        ch_near(s, 0, cl).start()
        for m in range(1, pairs):
            ch_far(s, m, cl).start()

        @pl.when(s > 0)
        def _():
            forward(s - 1)

        nn[...] = mm_nt(n_buf[s], n_buf[s])
        hh[...] = mm_nt(h_cli[s, cl], h_cli[s, cl])
        for k in range(1, line):
            rl_copy(s, k).wait_recv()
            summed = summed + line_buf[s, k - 1].astype(F32)
        o_buf[s, :, lanes(tp)] = summed.astype(BF16)

        ap_copy(s, 0, tp).start()
        for k in range(1, line):
            al_copy(s, k, tp).start()

        def arrived(p, first):
            at = lanes(p)
            block = o_buf[s, :, at]
            for ref, value in (
                (gh, mm_nt(block, wd_ref[:, at])),
                (oo, mm_nt(block, block)),
                (oh, mm_nt(block, o_hist[:, :, at].reshape(rows, dt))),
            ):
                ref[...] = value if first else ref[...] + value

        arrived(tp, True)
        for k in range(1, line):
            source = on_line(line - k) + side
            al_copy(s, k, source).wait_recv()
            ap_copy(s, k, source).start()
            arrived(source, False)
        for k in range(line):
            source = on_line(line - k) + 1 - side
            ap_copy(s, k, source).wait_recv()
            arrived(source, False)

        @pl.loop(1, n_cl)
        def _(k):
            co_copy(s, k, cl).start()

        sig = sg[...]
        gate = ga[...]
        grad_hidden = gh[...] + mm((oh[...] * coef[...]).astype(BF16), h_past())
        old_g, old_u = g_past(0), g_past(1)
        gg = (grad_hidden * ua[...] * (sig * (1.0 + gate * (1.0 - sig)))).astype(BF16)
        gu = (grad_hidden * (gate * sig)).astype(BF16)
        g_cli[0, s, cl] = gg
        g_cli[1, s, cl] = gu

        cg_near(s, 0, cl).start()
        for m in range(1, pairs):
            cg_far(s, m, cl).start()

        squares = sum_all(nn[...] * (mm_nt(gg, gg) + mm_nt(gu, gu)) + hh[...] * oo[...])
        sm_buf[s, tp, n_tp] = jnp.broadcast_to(squares, (1, dt))
        sm_buf[s, tp, n_tp + 1] = flag_ref[s]

        p_g = ((mm_nt(gg, old_g) + mm_nt(gu, old_u)) * coef[...]).astype(BF16)
        for p in range(n_tp):
            at = slice(p * dt, (p + 1) * dt)
            grad_normed = mm_nt(gg, wg_ref[at, :]) + mm_nt(gu, wu_ref[at, :])
            grad_normed = grad_normed + mm(p_g, n_buf[:past, :, at].reshape(rows, dt))
            sm_buf[s, tp, p] = jnp.sum(grad_normed * scaled[:, at], axis=0, keepdims=True)

        @pl.loop(1, n_tp)
        def _(k):
            sm_copy(s, k).start()

        @pl.when(s > 0)
        def _():
            add_out(s - 1)

        for k in range(line):
            rp_copy(s, k).wait_send()
            ap_copy(s, k, tp).wait_send()
        for k in range(1, line):
            rl_copy(s, k).wait_send()
            al_copy(s, k, tp).wait_send()

        @pl.loop(1, n_tp)
        def _(k):
            sm_arrival(s, k).wait_recv()

        total = sm_buf[s, 0]
        for t in range(1, n_tp):
            total = total + sm_buf[s, t]
        gain_grad = total[:n_tp]
        gain_square = jnp.sum(jnp.sum(gain_grad * gain_grad, axis=0), axis=1, keepdims=True)
        norm = jnp.sqrt(jnp.maximum(total[n_tp], 0.0) + gain_square + 1e-06)
        factor = jnp.where(total[n_tp + 1] < 0.5, limit / jnp.maximum(norm, limit), 0.0)
        fin[s, cl, n_tp] = factor

        @pl.when(s < past)
        def _():
            coef[:, pl.ds(pl.multiple_of(s * tok, tok), tok)] = factor[:, :tok] * (-LR)
            o_hist[s] = o_buf[s]

        for p in range(n_tp):
            change = factor * gain_grad[p]
            gain[p] = gain[p] - LR * change
            fin[s, cl, p] = change

        @pl.loop(1, n_cl)
        def _(k):
            fi_copy(s, k, cl).start()

        @pl.loop(1, n_tp)
        def _(k):
            sm_copy(s, k).wait_send()

        n_cli[s, cl] = n_buf[s, :, slice_of(cl)]
        o_cli[s, cl] = o_buf[s, :, slice_of(cl)]
        return carry

    lax.fori_loop(0, steps, step, 0)

    forward(steps - 1)
    add_out(steps - 1)
    for i in range(q):
        acc = jnp.zeros((1, dt), F32)
        for s in range(steps):
            for c in range(n_cl):
                acc = acc + fin[s, c, cl * q + i]
        ogain_ref[i] = acc * (1.0 / n_cl)

    @pl.loop(0, steps)
    def _(s):
        @pl.loop(1, n_cl)
        def _(k):
            cn_copy(s, k, cl).wait_send()
            co_copy(s, k, cl).wait_send()
            fi_copy(s, k, cl).wait_send()

        for m in range(pairs):
            ch_near(s, m, cl).wait_send()
            cg_near(s, m, cl).wait_send()
        for m in range(1, pairs):
            ch_far(s, m, cl).wait_send()
            cg_far(s, m, cl).wait_send()


def on_device(n_tp, n_cl, inputs, targets, norm_gain, gate_weight, up_weight, down_weight, overflow):
    tok, width = inputs.shape[1:]
    ff = gate_weight.shape[1]
    steps = overflow.shape[1]
    dt = width // n_tp
    ds = width // n_cl
    line = n_tp // 2
    limit = 0.5 * math.sqrt(3.0 * width * ff * n_tp)
    flags = jnp.broadcast_to(overflow.astype(F32).reshape(steps, 1, 1), (steps, 1, dt))
    gain = norm_gain.reshape(n_tp, 1, dt)
    dma = pltpu.SemaphoreType.DMA
    vmem = pl.BlockSpec(memory_space=pltpu.VMEM)
    gate, up, down, gain_out = pl.pallas_call(
        functools.partial(kernel, n_tp, n_cl, steps, limit),
        out_shape=(
            jax.ShapeDtypeStruct((ds, ff), F32),
            jax.ShapeDtypeStruct((ds, ff), F32),
            jax.ShapeDtypeStruct((ff, ds), F32),
            jax.ShapeDtypeStruct((ds // dt, 1, dt), F32),
        ),
        in_specs=[vmem] * 3 + [pl.BlockSpec(memory_space=pl.ANY)] * 3 + [vmem],
        out_specs=(vmem,) * 4,
        scratch_shapes=[
            pltpu.VMEM((width, ff), BF16),
            pltpu.VMEM((width, ff), BF16),
            pltpu.VMEM((ff, width), BF16),
            dma((3,)),
            pltpu.VMEM((steps - 1, tok, width), BF16),
            pltpu.VMEM((tok, width), F32),
            pltpu.VMEM((n_tp, 1, dt), F32),
            pltpu.VMEM((steps, tok, width), BF16),
            pltpu.VMEM((steps, tok, width), BF16),
            pltpu.VMEM((2, line, tok, dt), BF16),
            pltpu.VMEM((steps, line, tok, dt), BF16),
            pltpu.VMEM((steps, line - 1, tok, dt), BF16),
            pltpu.VMEM((steps, n_tp, n_tp + 2, 1, dt), F32),
            pltpu.VMEM((steps, n_cl, tok, ds), BF16),
            pltpu.VMEM((steps, n_cl, tok, ds), BF16),
            pltpu.VMEM((steps, n_cl, tok, ff), BF16),
            pltpu.VMEM((2, steps, n_cl, tok, ff), BF16),
            pltpu.VMEM((steps, n_cl, n_tp + 1, 1, dt), F32),
            pltpu.VMEM((tok, ff), F32),
            pltpu.VMEM((tok, ff), F32),
            pltpu.VMEM((tok, ff), F32),
            pltpu.VMEM((tok, ff), F32),
            pltpu.VMEM((tok, tok), F32),
            pltpu.VMEM((tok, tok), F32),
            pltpu.VMEM((tok, tok), F32),
            pltpu.VMEM((tok, (steps - 1) * tok), F32),
            pltpu.VMEM((1, (steps - 1) * tok), F32),
            dma((line,)), dma((steps, line)),
            dma((line - 1,)), dma((steps, line - 1)),
            dma((line,)), dma((steps, line)),
            dma((line - 1,)), dma((steps, line - 1)),
            dma((n_tp - 1,)), dma((steps, n_tp - 1)),
            dma((steps, n_cl - 1)), dma((steps, n_cl - 1)),
            dma((steps, n_cl - 1)), dma((steps, n_cl - 1)),
            dma((steps, n_cl - 1)), dma((steps, n_cl - 1)),
            dma((steps, n_cl - 1)), dma((steps, n_cl - 1)),
            dma((steps, n_cl - 1)), dma((steps, n_cl - 1)),
        ],
        compiler_params=pltpu.CompilerParams(
            collective_id=0, has_side_effects=True, vmem_limit_bytes=58 * 1024 * 1024
        ),
        name="fedavg_round",
    )(inputs[0], targets[0], gain, gate_weight, up_weight, down_weight, flags)
    return gate, up, down, gain_out.reshape(ds)


def solution(mesh):
    placed = (
        P("client", None, None),
        P("client", None, None),
        P(),
        P(None, "tp"),
        P(None, "tp"),
        P("tp", None),
        P("client", None, "tp"),
    )
    return jax.shard_map(
        functools.partial(on_device, mesh.shape["tp"], mesh.shape["client"]),
        mesh=mesh,
        in_specs=placed,
        out_specs=(P("client", "tp"), P("client", "tp"), P("tp", "client"), P("client")),
        check_vma=False,
    )
```

```python
import functools
import math

import jax
import jax.numpy as jnp
from jax import lax
from jax.experimental import pallas as pl
from jax.experimental.pallas import tpu as pltpu
from jax.sharding import PartitionSpec as P

LR = 0.005
F32 = jnp.float32
BF16 = jnp.bfloat16
MESH = pl.DeviceIdType.MESH


def mm(left, right):
    return lax.dot_general(left, right, (((1,), (0,)), ((), ())), preferred_element_type=F32)


def mm_nt(left, right):
    return lax.dot_general(left, right, (((1,), (1,)), ((), ())), preferred_element_type=F32)


def mm_tn(left, right):
    return lax.dot_general(left, right, (((0,), (0,)), ((), ())), preferred_element_type=F32)


def sum_all(value):
    return jnp.sum(jnp.sum(value, axis=0, keepdims=True), axis=1, keepdims=True)


def kernel(
    n_tp, n_cl, steps, limit,
    x_ref, t_ref, gain_ref, wg_hbm, wu_hbm, wd_hbm, flag_ref,
    og_ref, ou_ref, od_ref, ogain_ref,
    wg_ref, wu_ref, wd_ref, load, o_hist,
    scaled, gain, n_buf, o_buf, part, pair_buf, line_buf, sm_buf, n_cli, o_cli, h_cli, g_cli, fin,
    ga, ua, sg, gh, nn, hh, oo, oh, coef,
    rp_s, rp_r, rl_s, rl_r, ap_s, ap_r, al_s, al_r, sm_s, sm_r,
    cn_s, cn_r, ch_s, ch_r, co_s, co_r, cg_s, cg_r, fi_s, fi_r,
):
    tp = lax.axis_index("tp")
    cl = lax.axis_index("client")
    tok, width = x_ref.shape
    dt = width // n_tp
    ds = width // n_cl
    q = ds // dt

    def tp_peer(k):
        return lax.rem(tp + k, n_tp)

    def cl_peer(k):
        return lax.rem(cl + k, n_cl)

    loads = [
        pltpu.make_async_copy(src, dst, load.at[i])
        for i, (src, dst) in enumerate(((wg_hbm, wg_ref), (wu_hbm, wu_ref), (wd_hbm, wd_ref)))
    ]
    for copy in loads:
        copy.start()
    barrier = pltpu.get_barrier_semaphore()

    @pl.loop(1, n_tp)
    def _(k):
        pl.semaphore_signal(barrier, inc=1, device_id={"tp": tp_peer(k)}, device_id_type=MESH)

    @pl.loop(1, n_cl)
    def _(k):
        pl.semaphore_signal(barrier, inc=1, device_id={"client": cl_peer(k)}, device_id_type=MESH)

    def lanes(p):
        return pl.ds(pl.multiple_of(p * dt, dt), dt)

    def slice_of(c):
        return pl.ds(pl.multiple_of(c * ds, ds), ds)

    def tp_copy(src, dst, send, recv, k):
        return pltpu.make_async_remote_copy(
            src_ref=src, dst_ref=dst, send_sem=send, recv_sem=recv,
            device_id={"tp": tp_peer(k)}, device_id_type=MESH)

    def cl_copy(src, dst, send, recv, k):
        return pltpu.make_async_remote_copy(
            src_ref=src, dst_ref=dst, send_sem=send, recv_sem=recv,
            device_id={"client": cl_peer(k)}, device_id_type=MESH)

    line = n_tp // 2
    side = lax.rem(tp, 2)
    spot = lax.div(tp, 2)
    pair = tp + 1 - 2 * side
    sibling = cl + 1 - 2 * lax.rem(cl, 2)
    pairs = n_cl // 2

    def on_line(k):
        return lax.rem(spot + k, line) * 2

    def to_tp(src, dst, send, recv, peer):
        return pltpu.make_async_remote_copy(
            src_ref=src, dst_ref=dst, send_sem=send, recv_sem=recv,
            device_id={"tp": peer}, device_id_type=MESH)

    def to_cl(src, dst, send, recv, peer):
        return pltpu.make_async_remote_copy(
            src_ref=src, dst_ref=dst, send_sem=send, recv_sem=recv,
            device_id={"client": peer}, device_id_type=MESH)

    def rp_copy(s, k):
        return to_tp(part.at[0, k], pair_buf.at[s, k], rp_s.at[k], rp_r.at[s, k], pair)

    def rl_copy(s, k):
        return to_tp(part.at[1, k], line_buf.at[s, k - 1], rl_s.at[k - 1], rl_r.at[s, k - 1], on_line(k) + side)

    def al_copy(s, k, p):
        block = o_buf.at[s, :, lanes(p)]
        return to_tp(block, block, al_s.at[k - 1], al_r.at[s, k - 1], on_line(k) + side)

    def ap_copy(s, k, p):
        block = o_buf.at[s, :, lanes(p)]
        return to_tp(block, block, ap_s.at[k], ap_r.at[s, k], pair)

    def sm_copy(s, k):
        own = sm_buf.at[s, tp]
        return tp_copy(own, own, sm_s.at[k - 1], sm_r.at[s, k - 1], k)

    def sm_arrival(s, k):
        theirs = sm_buf.at[s, tp_peer(n_tp - k)]
        return tp_copy(theirs, theirs, sm_s.at[k - 1], sm_r.at[s, k - 1], k)

    def from_cl(k):
        return cl_peer(n_cl - k)

    def cn_copy(s, k, c):
        return cl_copy(n_buf.at[s, :, slice_of(cl_peer(k))], n_cli.at[s, c], cn_s.at[s, k - 1], cn_r.at[s, k - 1], k)

    def co_copy(s, k, c):
        return cl_copy(o_buf.at[s, :, slice_of(cl_peer(k))], o_cli.at[s, c], co_s.at[s, k - 1], co_r.at[s, k - 1], k)

    def far(m):
        return lax.rem(lax.div(cl, 2) + m, pairs) * 2 + lax.rem(cl, 2)

    def ch_far(s, m, c):
        block = h_cli.at[s, c]
        return to_cl(block, block, ch_s.at[s, m - 1], ch_r.at[s, m - 1], far(m))

    def ch_near(s, m, c):
        block = h_cli.at[s, c]
        return to_cl(block, block, ch_s.at[s, pairs - 1 + m], ch_r.at[s, pairs - 1 + m], sibling)

    def cg_far(s, m, c):
        block = g_cli.at[:, s, c]
        return to_cl(block, block, cg_s.at[s, m - 1], cg_r.at[s, m - 1], far(m))

    def cg_near(s, m, c):
        block = g_cli.at[:, s, c]
        return to_cl(block, block, cg_s.at[s, pairs - 1 + m], cg_r.at[s, pairs - 1 + m], sibling)

    def fi_copy(s, k, c):
        return cl_copy(fin.at[s, c], fin.at[s, c], fi_s.at[s, k - 1], fi_r.at[s, k - 1], k)

    def forward(s):
        for m in range(1, pairs):
            source = far(pairs - m)
            ch_far(s, m, source).wait_recv()
            ch_near(s, m, source).start()
            cg_far(s, m, source).wait_recv()
            cg_near(s, m, source).start()

    def add_out(s):
        for k in range(1, n_cl):
            c = from_cl(k)
            fi_copy(s, k, c).wait_recv()
            cn_copy(s, k, c).wait_recv()
            co_copy(s, k, c).wait_recv()
        for m in range(pairs):
            c = sibling if m == 0 else far(pairs - m) + 1 - 2 * lax.rem(cl, 2)
            ch_near(s, m, c).wait_recv()
            cg_near(s, m, c).wait_recv()
        for c in range(n_cl):
            f = fin[s, c, n_tp][:, :1] * (1.0 / n_cl)
            n_cli[s, c] = (n_cli[s, c].astype(F32) * f).astype(BF16)
            o_cli[s, c] = (o_cli[s, c].astype(F32) * f).astype(BF16)
        rows = n_cl * tok
        ff = wg_ref.shape[1]
        n_all = n_cli[s].reshape(rows, ds)
        og_ref[...] += mm_tn(n_all, g_cli[0, s].reshape(rows, ff))
        ou_ref[...] += mm_tn(n_all, g_cli[1, s].reshape(rows, ff))
        od_ref[...] += mm_tn(h_cli[s].reshape(rows, ff), o_cli[s].reshape(rows, ds))

    x = x_ref[...].astype(F32)
    scaled[...] = x * lax.rsqrt(jnp.mean(x * x, axis=-1, keepdims=True) + 1e-05)
    gain[...] = gain_ref[...]
    og_ref[...] = jnp.zeros_like(og_ref)
    ou_ref[...] = jnp.zeros_like(ou_ref)
    od_ref[...] = jnp.zeros_like(od_ref)
    past = steps - 1
    rows = past * tok
    ff = wg_ref.shape[1]
    coef[...] = jnp.zeros_like(coef)
    o_hist[...] = jnp.zeros_like(o_hist)
    for j in range(past):
        n_buf[j] = jnp.zeros((tok, width), BF16)
        h_cli[j, cl] = jnp.zeros((tok, ff), BF16)
        g_cli[0, j, cl] = jnp.zeros((tok, ff), BF16)
        g_cli[1, j, cl] = jnp.zeros((tok, ff), BF16)
    for copy in loads:
        copy.wait()

    def h_past():
        return h_cli[:past, cl].reshape(rows, ff)

    def g_past(i):
        return g_cli[i, :past, cl].reshape(rows, ff)

    def step(s, carry):
        for p in range(n_tp):
            at = slice(p * dt, (p + 1) * dt)
            n_buf[s, :, at] = (scaled[:, at] * gain[p]).astype(BF16)

        @pl.when(s == 0)
        def _():
            pl.semaphore_wait(barrier, n_tp - 1 + n_cl - 1)

        @pl.loop(1, n_cl)
        def _(k):
            cn_copy(s, k, cl).start()

        normed = n_buf[s]
        ga[...] = mm(normed, wg_ref[...])
        ua[...] = mm(normed, wu_ref[...])

        @pl.when(s > 0)
        def _():
            p = (mm_nt(n_buf[s], n_buf[:past].reshape(rows, width)) * coef[...]).astype(BF16)
            ga[...] += mm(p, g_past(0))
            ua[...] += mm(p, g_past(1))

        gate = ga[...]
        sig = jax.nn.sigmoid(gate)
        silu = gate * sig
        sg[...] = sig
        hidden = (silu * ua[...]).astype(BF16)
        h_cli[s, cl] = hidden
        p_h = (mm_nt(hidden, h_past()) * coef[...]).astype(BF16)

        def out_chunk(p):
            at = lanes(p)
            return mm(hidden, wd_ref[:, at]) + mm(p_h, o_hist[:, :, at].reshape(rows, dt))

        order = list(range(1, line)) + [0]
        for k in order:
            part[0, k] = out_chunk(on_line(k) + 1 - side).astype(BF16)
            rp_copy(s, k).start()
        for k in order:
            summed = out_chunk(on_line(k) + side)
            rp_copy(s, k).wait_recv()
            summed = summed + pair_buf[s, k].astype(F32)
            if k > 0:
                part[1, k] = summed.astype(BF16)
                rl_copy(s, k).start()

        summed = summed + (x_ref[:, lanes(tp)].astype(F32) - t_ref[:, lanes(tp)].astype(F32))
        ch_near(s, 0, cl).start()
        for m in range(1, pairs):
            ch_far(s, m, cl).start()

        @pl.when(s > 0)
        def _():
            forward(s - 1)

        nn[...] = mm_nt(n_buf[s], n_buf[s])
        hh[...] = mm_nt(h_cli[s, cl], h_cli[s, cl])
        for k in range(1, line):
            rl_copy(s, k).wait_recv()
            summed = summed + line_buf[s, k - 1].astype(F32)
        o_buf[s, :, lanes(tp)] = summed.astype(BF16)

        ap_copy(s, 0, tp).start()
        for k in range(1, line):
            al_copy(s, k, tp).start()

        def arrived(p, first):
            at = lanes(p)
            block = o_buf[s, :, at]
            for ref, value in (
                (gh, mm_nt(block, wd_ref[:, at])),
                (oo, mm_nt(block, block)),
                (oh, mm_nt(block, o_hist[:, :, at].reshape(rows, dt))),
            ):
                ref[...] = value if first else ref[...] + value

        arrived(tp, True)
        for k in range(1, line):
            source = on_line(line - k) + side
            al_copy(s, k, source).wait_recv()
            ap_copy(s, k, source).start()
            arrived(source, False)
        for k in range(line):
            source = on_line(line - k) + 1 - side
            ap_copy(s, k, source).wait_recv()
            arrived(source, False)

        @pl.loop(1, n_cl)
        def _(k):
            co_copy(s, k, cl).start()

        sig = sg[...]
        gate = ga[...]
        grad_hidden = gh[...] + mm((oh[...] * coef[...]).astype(BF16), h_past())
        old_g, old_u = g_past(0), g_past(1)
        gg = (grad_hidden * ua[...] * (sig * (1.0 + gate * (1.0 - sig)))).astype(BF16)
        gu = (grad_hidden * (gate * sig)).astype(BF16)
        g_cli[0, s, cl] = gg
        g_cli[1, s, cl] = gu

        cg_near(s, 0, cl).start()
        for m in range(1, pairs):
            cg_far(s, m, cl).start()

        squares = sum_all(nn[...] * (mm_nt(gg, gg) + mm_nt(gu, gu)) + hh[...] * oo[...])
        sm_buf[s, tp, n_tp] = jnp.broadcast_to(squares, (1, dt))
        sm_buf[s, tp, n_tp + 1] = jnp.full((1, dt), flag_ref[s], jnp.int32).astype(F32)

        p_g = ((mm_nt(gg, old_g) + mm_nt(gu, old_u)) * coef[...]).astype(BF16)
        for p in range(n_tp):
            at = slice(p * dt, (p + 1) * dt)
            grad_normed = mm_nt(gg, wg_ref[at, :]) + mm_nt(gu, wu_ref[at, :])
            grad_normed = grad_normed + mm(p_g, n_buf[:past, :, at].reshape(rows, dt))
            sm_buf[s, tp, p] = jnp.sum(grad_normed * scaled[:, at], axis=0, keepdims=True)

        @pl.loop(1, n_tp)
        def _(k):
            sm_copy(s, k).start()

        @pl.when(s > 0)
        def _():
            add_out(s - 1)

        n_cli[s, cl] = n_buf[s, :, slice_of(cl)]
        o_cli[s, cl] = o_buf[s, :, slice_of(cl)]

        @pl.when(s < past)
        def _():
            o_hist[s] = o_buf[s]

        @pl.when(s == past)
        def _():
            forward(s)

        for k in range(line):
            rp_copy(s, k).wait_send()
            ap_copy(s, k, tp).wait_send()
        for k in range(1, line):
            rl_copy(s, k).wait_send()
            al_copy(s, k, tp).wait_send()

        @pl.loop(1, n_tp)
        def _(k):
            sm_arrival(s, k).wait_recv()

        total = sm_buf[s, 0]
        for t in range(1, n_tp):
            total = total + sm_buf[s, t]
        gain_grad = total[:n_tp]
        gain_square = jnp.sum(jnp.sum(gain_grad * gain_grad, axis=0), axis=1, keepdims=True)
        norm = jnp.sqrt(jnp.maximum(total[n_tp], 0.0) + gain_square + 1e-06)
        factor = jnp.where(total[n_tp + 1] < 0.5, limit / jnp.maximum(norm, limit), 0.0)
        fin[s, cl, n_tp] = factor

        @pl.when(s < past)
        def _():
            coef[:, pl.ds(pl.multiple_of(s * tok, tok), tok)] = factor[:, :tok] * (-LR)

        for p in range(n_tp):
            change = factor * gain_grad[p]
            gain[p] = gain[p] - LR * change
            fin[s, cl, p] = change

        @pl.loop(1, n_cl)
        def _(k):
            fi_copy(s, k, cl).start()

        @pl.loop(1, n_tp)
        def _(k):
            sm_copy(s, k).wait_send()

        return carry

    lax.fori_loop(0, steps, step, 0)

    add_out(steps - 1)
    for i in range(q):
        acc = jnp.zeros((1, dt), F32)
        for s in range(steps):
            for c in range(n_cl):
                acc = acc + fin[s, c, cl * q + i]
        ogain_ref[i] = acc * (1.0 / n_cl)

    @pl.loop(0, steps)
    def _(s):
        @pl.loop(1, n_cl)
        def _(k):
            cn_copy(s, k, cl).wait_send()
            co_copy(s, k, cl).wait_send()
            fi_copy(s, k, cl).wait_send()

        for m in range(pairs):
            ch_near(s, m, cl).wait_send()
            cg_near(s, m, cl).wait_send()
        for m in range(1, pairs):
            ch_far(s, m, cl).wait_send()
            cg_far(s, m, cl).wait_send()


def on_device(n_tp, n_cl, inputs, targets, norm_gain, gate_weight, up_weight, down_weight, overflow):
    tok, width = inputs.shape[1:]
    ff = gate_weight.shape[1]
    steps = overflow.shape[1]
    dt = width // n_tp
    ds = width // n_cl
    line = n_tp // 2
    limit = 0.5 * math.sqrt(3.0 * width * ff * n_tp)
    gain = norm_gain.reshape(n_tp, 1, dt)
    dma = pltpu.SemaphoreType.DMA
    vmem = pl.BlockSpec(memory_space=pltpu.VMEM)
    gate, up, down, gain_out = pl.pallas_call(
        functools.partial(kernel, n_tp, n_cl, steps, limit),
        out_shape=(
            jax.ShapeDtypeStruct((ds, ff), F32),
            jax.ShapeDtypeStruct((ds, ff), F32),
            jax.ShapeDtypeStruct((ff, ds), F32),
            jax.ShapeDtypeStruct((ds // dt, 1, dt), F32),
        ),
        in_specs=[vmem] * 3 + [pl.BlockSpec(memory_space=pl.ANY)] * 3
        + [pl.BlockSpec(memory_space=pltpu.SMEM)],
        out_specs=(vmem,) * 4,
        scratch_shapes=[
            pltpu.VMEM((width, ff), BF16),
            pltpu.VMEM((width, ff), BF16),
            pltpu.VMEM((ff, width), BF16),
            dma((3,)),
            pltpu.VMEM((steps - 1, tok, width), BF16),
            pltpu.VMEM((tok, width), F32),
            pltpu.VMEM((n_tp, 1, dt), F32),
            pltpu.VMEM((steps, tok, width), BF16),
            pltpu.VMEM((steps, tok, width), BF16),
            pltpu.VMEM((2, line, tok, dt), BF16),
            pltpu.VMEM((steps, line, tok, dt), BF16),
            pltpu.VMEM((steps, line - 1, tok, dt), BF16),
            pltpu.VMEM((steps, n_tp, n_tp + 2, 1, dt), F32),
            pltpu.VMEM((steps, n_cl, tok, ds), BF16),
            pltpu.VMEM((steps, n_cl, tok, ds), BF16),
            pltpu.VMEM((steps, n_cl, tok, ff), BF16),
            pltpu.VMEM((2, steps, n_cl, tok, ff), BF16),
            pltpu.VMEM((steps, n_cl, n_tp + 1, 1, dt), F32),
            pltpu.VMEM((tok, ff), F32),
            pltpu.VMEM((tok, ff), F32),
            pltpu.VMEM((tok, ff), F32),
            pltpu.VMEM((tok, ff), F32),
            pltpu.VMEM((tok, tok), F32),
            pltpu.VMEM((tok, tok), F32),
            pltpu.VMEM((tok, tok), F32),
            pltpu.VMEM((tok, (steps - 1) * tok), F32),
            pltpu.VMEM((1, (steps - 1) * tok), F32),
            dma((line,)), dma((steps, line)),
            dma((line - 1,)), dma((steps, line - 1)),
            dma((line,)), dma((steps, line)),
            dma((line - 1,)), dma((steps, line - 1)),
            dma((n_tp - 1,)), dma((steps, n_tp - 1)),
            dma((steps, n_cl - 1)), dma((steps, n_cl - 1)),
            dma((steps, n_cl - 1)), dma((steps, n_cl - 1)),
            dma((steps, n_cl - 1)), dma((steps, n_cl - 1)),
            dma((steps, n_cl - 1)), dma((steps, n_cl - 1)),
            dma((steps, n_cl - 1)), dma((steps, n_cl - 1)),
        ],
        compiler_params=pltpu.CompilerParams(
            collective_id=0, has_side_effects=True, vmem_limit_bytes=58 * 1024 * 1024
        ),
        name="fedavg_round",
    )(inputs[0], targets[0], gain, gate_weight, up_weight, down_weight, overflow.reshape(steps))
    return gate, up, down, gain_out.reshape(ds)


def solution(mesh):
    placed = (
        P("client", None, None),
        P("client", None, None),
        P(),
        P(None, "tp"),
        P(None, "tp"),
        P("tp", None),
        P("client", None, "tp"),
    )
    return jax.shard_map(
        functools.partial(on_device, mesh.shape["tp"], mesh.shape["client"]),
        mesh=mesh,
        in_specs=placed,
        out_specs=(P("client", "tp"), P("client", "tp"), P("tp", "client"), P("client")),
        check_vma=False,
    )
```
